32 devices in a mesh: grp: 4 (over z), lat: 8 (over y, x, core).
Axes of the slice: x: 2, y: 2, z: 4, core: 2. Of those that a mesh axis runs over, the one named last changes fastest.
Arguments:
- stream: bfloat16 [256, 8192], P('lat'), may hold values from -26 to 26
- batch_index: int32 [256], replicated, may hold values from 0 to 255
- weight: bfloat16 [8192, 4096], P(None, ('grp', 'lat')), may hold values from -0.26516504 to 0.26516504
- enc_bias: float32 [4096], P(('grp', 'lat')), may hold values from -1.5 to 0.5
- dec_bias: float32 [8192], replicated, may hold values from -3 to 3
Outputs:
- weight_grad: bfloat16 [8192, 4096], P(None, ('grp', 'lat'))
- bias_grad: float32 [4096], P(('grp', 'lat'))
- recon_error: bfloat16 [256, 8192], P('lat')
The draws below stay inside these ranges and needn't reach their ends.
All inputs are finite; a program needn't handle non-finite values.
Results may differ from the reference program's by a relative error of at most 0.025.
Values may be sent and summed in bfloat16 or wider, within the bound.
A program may use at most 64 MiB of HBM per device.

```python
import math
import jax
import jax.numpy as jnp
from jax import lax

D = 8192
LAT_DEV = 128
TOKENS = 256
LATENTS = 4096
RUNS = 32


def draw_stream(key, part):
    level = jnp.arange(TOKENS).astype(jnp.float32) / max(TOKENS - 1, 1)
    growth = jnp.exp(0.5 * math.log(3.0) * level)
    values = jnp.clip(jax.random.normal(key, (TOKENS, D), jnp.float32), -5.0, 5.0)
    return (values * growth[:, None]).astype(jnp.bfloat16)


def draw_weight(key, part):
    first_key, second_key = jax.random.split(key, 2)
    values = jnp.clip(jax.random.normal(first_key, (D, LATENTS), jnp.float32), -6.0, 6.0)
    spread = math.log(2.0)
    level = jnp.arange(LATENTS).astype(jnp.float32) / max(LATENTS - 1, 1)
    growth = jnp.exp(0.5 * math.log(3.0) * level)[None, :]
    column_scale = jnp.exp(jax.random.uniform(second_key, (1, LATENTS), jnp.float32, -spread, spread))
    return (values * column_scale * growth / math.sqrt(D)).astype(jnp.bfloat16)


def plant(values, key, low, high):
    dims = values.shape
    place = [jax.random.randint(jax.random.fold_in(key, axis), (), 0, dims[axis]) for axis in range(len(dims))]
    values = values.at[tuple(place)].set(low)
    longest = dims.index(max(dims))
    place[longest] = (place[longest] + 1) % dims[longest]
    return values.at[tuple(place)].set(high)


def shard_levels(own_key, dims, cuts, smallest, high):
    level, own = 1.0, jax.random.fold_in(own_key, 6)
    for axis_at, shards_of in cuts:
        draws = jnp.exp(jax.random.uniform(jax.random.fold_in(own, axis_at), (shards_of,), jnp.float32, smallest / len(cuts), high / len(cuts)))
        level = level * jnp.repeat(draws, dims[axis_at] // shards_of).reshape([-1 if axis == axis_at else 1 for axis in range(len(dims))])
    return level


def noise(own_key, shape, width, reach, kind=jnp.bfloat16):
    result = width * jax.random.normal(own_key, shape, jnp.float32)
    return jnp.clip(result, min=-reach, max=reach).astype(kind)


def setup_inputs(seed: int = 0) -> dict:
    key_of = jax.random.split(jax.random.key(seed), 6)
    return {
        "stream": draw_stream(jax.random.fold_in(key_of[5], 71), 0),
        "batch_index": plant(jax.random.randint(key_of[1], (TOKENS,), 0, TOKENS), jax.random.fold_in(key_of[1], 1), 0, TOKENS - 1).astype(jnp.int32),
        "weight": draw_weight(jax.random.fold_in(key_of[5], 71), 0),
        "enc_bias": jnp.clip(-1.5 + 2.0 * jax.random.uniform(key_of[3], (LATENTS,), jnp.float32) ** shard_levels(key_of[3], (LATENTS,), ((0, 32),), -0.2, 0.2), -1.5, 0.5),
        "dec_bias": noise(key_of[4], (D,), 0.5, 3.0, jnp.float32),
    }


sharpness = 8.0
penalty = 0.25
epsilon = 1e-06

def run_columns(weight, enc_bias, run):
    start = (run * LAT_DEV).astype(jnp.int32)
    columns = lax.dynamic_slice_in_dim(weight, start, LAT_DEV, 1)
    biases = lax.dynamic_slice_in_dim(enc_bias, start, LAT_DEV, 0)
    return (columns, biases)

def reference(stream, batch_index, weight, enc_bias, dec_bias):
    batch = jnp.take(stream, batch_index, axis=0)
    centered = (batch.astype(jnp.float32) - dec_bias).astype(jnp.bfloat16)
    runs = jnp.arange(RUNS, dtype=jnp.int32)

    def forward_run(centered_rows, run):
        columns, biases = run_columns(weight, enc_bias, run)
        preact = jnp.dot(centered_rows, columns, preferred_element_type=jnp.float32) + biases
        active = (jax.nn.softplus(sharpness * preact) / sharpness).astype(jnp.bfloat16)
        return (columns, preact, active)

    def add_run(running, run):
        columns, preact, active = forward_run(centered, run)
        term = lax.dot_general(active, columns, (((1,), (1,)), ((), ())), preferred_element_type=jnp.float32)
        rounded = lax.optimization_barrier(term.astype(jnp.bfloat16)).astype(jnp.float32)
        return (running + rounded, None)
    summed, _ = lax.scan(add_run, jnp.zeros((TOKENS, D), jnp.float32), runs)
    error = summed + dec_bias - batch.astype(jnp.float32)
    grad_rows = (2.0 * error).astype(jnp.bfloat16)

    def grad_run(run):
        columns, preact, active = forward_run(centered, run)
        grad_active = jnp.dot(grad_rows, columns, preferred_element_type=jnp.float32) + penalty
        grad_pre = grad_active * jax.nn.sigmoid(sharpness * preact)
        grad_raw = lax.dot_general(centered, grad_pre.astype(jnp.bfloat16), (((0,), (0,)), ((), ())), preferred_element_type=jnp.float32)
        grad_raw = grad_raw + lax.dot_general(grad_rows, active, (((0,), (0,)), ((), ())), preferred_element_type=jnp.float32)
        return (grad_raw, lax.optimization_barrier(jnp.sum(grad_pre, axis=0)))

    def add_squares(total, run):
        grad_raw, bias_raw = grad_run(run)
        return (total + jnp.sum(grad_raw * grad_raw) + jnp.sum(bias_raw * bias_raw), bias_raw)
    total_sq, bias_raw = lax.scan(add_squares, jnp.zeros((), jnp.float32), runs)
    factor = jnp.minimum(1.0, 1.0 / jnp.sqrt(total_sq / ((D + 1) * LATENTS) + epsilon))

    def scaled_run(run):
        grad_raw, _ = grad_run(run)
        return (grad_raw * factor).astype(jnp.bfloat16)
    weight_grad = lax.map(scaled_run, runs).transpose(1, 0, 2).reshape(D, LATENTS)
    bias_grad = (bias_raw * factor).reshape(LATENTS)
    return (weight_grad, bias_grad, error.astype(jnp.bfloat16))
```

```python
import functools

import jax
import jax.numpy as jnp
from jax import lax
from jax.experimental import pallas as pl
from jax.experimental.pallas import tpu as pltpu
from jax.sharding import PartitionSpec as P

sharpness = 8.0
penalty = 0.25
epsilon = 1e-06
f32 = jnp.float32
bf16 = jnp.bfloat16
MESH = pl.DeviceIdType.MESH


def chunk_of(length, most):
    return next(c for c in range(min(most, length), 0, -16) if length % c == 0)


def bit_orders(n_lat, n_grp):
    lat_bits = n_lat.bit_length() - 1
    grp_bits = n_grp.bit_length() - 1
    x_bits = (lat_bits - 1) // 2
    core = [("lat", 1)]
    x = [("lat", 1 << b) for b in range(1, 1 + x_bits)]
    y = [("lat", 1 << b) for b in range(1 + x_bits, lat_bits)]
    z = [("grp", 1 << b) for b in range(grp_bits)]
    return core, x, y, z


def kernel(n_lat, n_grp, stream_ref, idx_row_ref, idx_col_ref, weight_ref, enc_ref, dec_ref,
           wgrad_ref, bias_ref, err_ref,
           gathered, centered_t, weight_t, part, landed, grad_t, raw, tiles,
           gs_sem, gr_sem, rs_sem, rr_sem, as_sem, ar_sem, ts_sem, tr_sem):
    rows, width = stream_ref.shape
    tokens = idx_row_ref.shape[1]
    n = n_lat * n_grp
    me = {"lat": lax.axis_index("lat"), "grp": lax.axis_index("grp")}
    core, x, y, z = bit_orders(n_lat, n_grp)
    everyone = core + x + y + z

    def partner(bit):
        axis, mask = bit
        return {a: (jnp.bitwise_xor(me[a], mask) if a == axis else me[a]) for a in ("grp", "lat")}

    def side(bit):
        axis, mask = bit
        return jnp.bitwise_and(jnp.right_shift(me[axis], mask.bit_length() - 1), 1)

    def send(src, dst, send_sem, recv_sem, bit):
        copy = pltpu.make_async_remote_copy(
            src_ref=src, dst_ref=dst, send_sem=send_sem, recv_sem=recv_sem,
            device_id=partner(bit), device_id_type=MESH)
        copy.start()
        return copy

    barrier = pltpu.get_barrier_semaphore()
    for bit in everyone:
        pl.semaphore_signal(barrier, inc=1, device_id=partner(bit), device_id_type=MESH)
    pl.semaphore_wait(barrier, len(everyone))

    half = width // 2
    flows = []
    for p, order in enumerate((x + y + core, y + x + core)):
        flows.append((pl.ds(p * half, half), [mask for _, mask in order]))
    gathers = [{}, {}]

    def forward(p, m, later):
        cols, order = flows[p]
        rank = jnp.bitwise_xor(me["lat"], m)
        src = stream_ref.at[:, cols] if m == 0 else gathered.at[rank, :, cols]
        for mask in later:
            gathers[p][m | mask] = send(
                src, gathered.at[rank, :, cols], gs_sem.at[p, m | mask], gr_sem.at[p, m | mask], ("lat", mask))

    span = [0]
    for p in (0, 1):
        forward(p, 0, flows[p][1])
    own_copy = pltpu.make_async_copy(stream_ref, gathered.at[me["lat"]], gs_sem.at[0, 0])
    own_copy.start()

    c = chunk_of(width, 512)
    for at in range(0, width, c):
        weight_t[:, at:at + c] = weight_ref[at:at + c, :].T
    square = (tokens, tokens)
    hits = (lax.broadcasted_iota(jnp.int32, square, 0) == idx_row_ref[...]).astype(f32)
    count = jnp.sum(hits, axis=1, keepdims=True)

    spans = [[0], [0]]
    for stage in range(len(flows[0][1])):
        fresh = []
        for p in (0, 1):
            order = flows[p][1]
            for m in spans[p]:
                fresh.append((p, m | order[stage]))
        for p, m in fresh:
            gathers[p][m].wait_recv()
            forward(p, m, flows[p][1][stage + 1:])
            spans[p].append(m)
    own_copy.wait()

    preact = jnp.zeros((tokens, weight_ref.shape[1]), f32)

    def center(at, c):
        block = gathered[:, :, at:at + c].astype(f32).reshape(tokens, c)
        return (block - dec_ref[:, at:at + c]).astype(bf16)

    for at in range(0, width, c):
        preact = preact + jnp.dot(center(at, c), weight_ref[at:at + c, :], preferred_element_type=f32)
    preact = preact + enc_ref[...]
    sharp = sharpness * preact
    active32 = (jnp.maximum(sharp, 0.0) + jnp.log1p(jnp.exp(-jnp.abs(sharp)))) / sharpness
    active = active32.astype(bf16)

    units = width // (16 * n)
    if units >= 8:
        small = units // 4
        big = (units - small) // 2
        small = units - 2 * big
        parts = [(big, core + x + y + z), (big, core + y + x + z), (small, core + z + x + y)]
    else:
        parts = [(units, core + x + y + z)]
    base, plan = 0, []
    for size, order in parts:
        plan.append((base, size * 16 * n, order))
        base += size * 16 * n
    n_bits = len(everyone)

    def aligned(at):
        return pl.multiple_of(at, 16)

    def term(at, length):
        c = chunk_of(length, 512)
        for k in range(0, length, c):
            here = pl.ds(aligned(at + k), c)
            part[here, :] = lax.dot_general(
                weight_ref[here, :], active, (((1,), (1,)), ((), ())), preferred_element_type=f32).astype(bf16)

    def over(length, most, step):
        c = chunk_of(length, most)
        if length == c:
            step(0, c)
        else:
            @pl.loop(0, length // c)
            def _(k):
                step(aligned(k * c), c)

    where, room = [], 0
    sends = []
    copies = {}
    for p, (start, length, order) in enumerate(plan):
        stay = aligned(start + side(order[0]) * (length // 2))
        go = aligned(start + (1 - side(order[0])) * (length // 2))
        term(go, length // 2)
        spot = room
        room += length // 2
        copies[p] = send(part.at[pl.ds(go, length // 2), :], landed.at[pl.ds(spot, length // 2), :],
                         rs_sem.at[p, 0], rr_sem.at[p, 0], order[0])
        sends.append(copies[p])
        where.append([stay, length // 2, spot])
    for p in range(len(plan)):
        term(where[p][0], where[p][1])

    for stage in range(1, n_bits):
        for p, (_, _, order) in enumerate(plan):
            at, length, spot = where[p]
            copies[p].wait_recv()
            now = length // 2
            stay_by = side(order[stage]) * now
            go_by = (1 - side(order[stage])) * now

            def add(by):
                def step(k, c):
                    here = pl.ds(aligned(at + by + k), c)
                    part[here, :] = (part[here, :].astype(f32)
                                     + landed[pl.ds(aligned(spot + by + k), c), :].astype(f32)).astype(bf16)
                over(now, 128, step)

            add(go_by)
            next_spot = room
            room += now
            copies[p] = send(part.at[pl.ds(aligned(at + go_by), now), :], landed.at[pl.ds(next_spot, now), :],
                             rs_sem.at[p, stage], rr_sem.at[p, stage], order[stage])
            sends.append(copies[p])
            add(stay_by)
            where[p] = [aligned(at + stay_by), now, next_spot]
        if stage == 1:
            for k in range(0, width, c):
                centered_t[k:k + c, :] = center(k, c).T

    for p, (_, _, order) in enumerate(plan):
        at, length, spot = where[p]
        copies[p].wait_recv()

        def finish(k, c):
            here = pl.ds(aligned(at + k), c)
            total = part[here, :].astype(f32) + landed[pl.ds(aligned(spot + k), c), :].astype(f32)
            grad_t[here, :] = (2.0 * (total - centered_t[here, :].astype(f32))).astype(bf16)
        over(length, 128, finish)

    for stage in reversed(range(n_bits)):
        for p, (_, _, order) in enumerate(plan):
            at, length, _ = where[p]
            if stage < n_bits - 1:
                copies[p].wait_recv()
            region = grad_t.at[pl.ds(at, length), :]
            copies[p] = send(region, region, as_sem.at[p, stage], ar_sem.at[p, stage], order[stage])
            sends.append(copies[p])
            where[p] = [aligned(at - side(order[stage]) * length), 2 * length, 0]
    for p in range(len(plan)):
        copies[p].wait_recv()

    grad_active_t = jnp.zeros((weight_ref.shape[1], tokens), f32)
    for k in range(0, width, c):
        grad_active_t = grad_active_t + jnp.dot(weight_t[:, k:k + c], grad_t[k:k + c, :], preferred_element_type=f32)
    grad_pre = (grad_active_t.T + penalty) * jax.nn.sigmoid(sharp) * count
    bias_raw = jnp.sum(grad_pre, axis=0, keepdims=True)
    pre16 = grad_pre.astype(bf16)
    drawn = (active32 * count).astype(bf16)
    squares = jnp.zeros((8, weight_ref.shape[1]), f32)
    for k in range(0, width, c):
        block = (jnp.dot(centered_t[k:k + c, :], pre16, preferred_element_type=f32)
                 + jnp.dot(grad_t[k:k + c, :], drawn, preferred_element_type=f32))
        raw[k:k + c, :] = block
        squares = squares + jnp.sum((block * block).reshape(c // 8, 8, block.shape[1]), axis=0)
    first = lax.broadcasted_iota(jnp.int32, squares.shape, 0) == 0
    squares = squares + jnp.where(first, bias_raw * bias_raw, 0.0)

    tiles[0] = squares
    own = idx_col_ref[pl.ds(pl.multiple_of(me["lat"] * rows, 8), rows), :]
    pick = (lax.broadcasted_iota(jnp.int32, (rows, tokens), 1) == own).astype(bf16)
    for i, bit in enumerate(everyone):
        copy = send(tiles.at[2 * i], tiles.at[2 * i + 1], ts_sem.at[i], tr_sem.at[i], bit)
        sends.append(copy)
        if i == 0:
            for k in range(0, width, c):
                rows_of = lax.dot_general(pick, grad_t[k:k + c, :], (((1,), (1,)), ((), ())), preferred_element_type=f32)
                err_ref[:, k:k + c] = (0.5 * rows_of).astype(bf16)
        copy.wait_recv()
        tiles[2 * i + 2] = tiles[2 * i] + tiles[2 * i + 1]
    total = jnp.sum(tiles[2 * n_bits])
    entries = (width + 1) * weight_ref.shape[1] * n
    mean = jnp.full((1, weight_ref.shape[1]), total / entries + epsilon, f32)
    factor = jnp.minimum(1.0, 1.0 / jnp.sqrt(mean))
    bias_ref[...] = bias_raw * factor
    for k in range(0, width, c):
        wgrad_ref[k:k + c, :] = (raw[k:k + c, :] * factor).astype(bf16)

    for copy in sends:
        copy.wait_send()
    for p in (0, 1):
        for m in sorted(gathers[p]):
            gathers[p][m].wait_send()


def body(n_lat, n_grp, stream, batch_index, weight, enc_bias, dec_bias):
    rows, width = stream.shape
    tokens = batch_index.shape[0]
    latents = weight.shape[1]
    n_bits = (n_lat * n_grp).bit_length() - 1
    vmem = pl.BlockSpec(memory_space=pltpu.VMEM)
    dma = pltpu.SemaphoreType.DMA
    weight_grad, bias_grad, error = pl.pallas_call(
        functools.partial(kernel, n_lat, n_grp),
        out_shape=(
            jax.ShapeDtypeStruct(weight.shape, bf16),
            jax.ShapeDtypeStruct((1, latents), f32),
            jax.ShapeDtypeStruct((rows, width), bf16),
        ),
        in_specs=[vmem] * 6,
        out_specs=(vmem, vmem, vmem),
        scratch_shapes=[
            pltpu.VMEM((n_lat, rows, width), bf16),
            pltpu.VMEM((width, tokens), bf16),
            pltpu.VMEM((latents, width), bf16),
            pltpu.VMEM((width, tokens), bf16),
            pltpu.VMEM((width, tokens), bf16),
            pltpu.VMEM((width, tokens), bf16),
            pltpu.VMEM((width, latents), f32),
            pltpu.VMEM((2 * n_bits + 1, 8, latents), f32),
            dma((2, n_lat)),
            dma((2, n_lat)),
            dma((3, n_bits)),
            dma((3, n_bits)),
            dma((3, n_bits)),
            dma((3, n_bits)),
            dma((n_bits,)),
            dma((n_bits,)),
        ],
        compiler_params=pltpu.CompilerParams(
            collective_id=0, has_side_effects=True, vmem_limit_bytes=56 * 1024 * 1024),
        cost_estimate=pl.CostEstimate(
            flops=2 * tokens * width * latents * 5, bytes_accessed=8 * width * latents, transcendentals=0),
    )(
        stream,
        batch_index.reshape(1, tokens),
        batch_index.reshape(tokens, 1),
        weight,
        enc_bias.reshape(1, latents),
        dec_bias.reshape(1, width),
    )
    return weight_grad, bias_grad.reshape(latents), error


def solution(mesh):
    return jax.shard_map(
        functools.partial(body, mesh.shape["lat"], mesh.shape["grp"]),
        mesh=mesh,
        in_specs=(P("lat", None), P(), P(None, ("grp", "lat")), P(("grp", "lat")), P()),
        out_specs=(P(None, ("grp", "lat")), P(("grp", "lat")), P("lat", None)),
        check_vma=False,
    )
```

```python
import functools

import jax
import jax.numpy as jnp
from jax import lax
from jax.experimental import pallas as pl
from jax.experimental.pallas import tpu as pltpu
from jax.sharding import PartitionSpec as P

sharpness = 8.0
penalty = 0.25
epsilon = 1e-06
f32 = jnp.float32
bf16 = jnp.bfloat16
MESH = pl.DeviceIdType.MESH


def chunk_of(length, most):
    return next(c for c in range(min(most, length), 0, -16) if length % c == 0)


def bit_orders(n_lat, n_grp):
    lat_bits = n_lat.bit_length() - 1
    grp_bits = n_grp.bit_length() - 1
    x_bits = (lat_bits - 1) // 2
    core = [("lat", 1)]
    x = [("lat", 1 << b) for b in range(1, 1 + x_bits)]
    y = [("lat", 1 << b) for b in range(1 + x_bits, lat_bits)]
    z = [("grp", 1 << b) for b in range(grp_bits)]
    return core, x, y, z


def split(units, core, x, y, z):
    if units < 16:
        return [(units, core + x + y + z)]
    once = [(3, core + x + y + z), (3, core + y + x + z), (2, core + z + x + y)]
    return [(size * units // 16, order) for size, order in once * 2]


def kernel(n_lat, n_grp, n_parts, stream_ref, idx_ref, weight_ref, enc_ref, dec_ref,
           raw_ref, bias_ref, factor_ref, err_ref,
           gathered, centered, centered_t, weight_t, part, landed, grad_t, raw, hits_t, lat_tiles, grp_tiles,
           gs_sem, gr_sem, rs_sem, rr_sem, as_sem, ar_sem, ls_sem, lr_sem, zs_sem, zr_sem, out_sem):
    rows, width = stream_ref.shape
    tokens = idx_ref.shape[1]
    n = n_lat * n_grp
    me = {"lat": lax.axis_index("lat"), "grp": lax.axis_index("grp")}
    core, x, y, z = bit_orders(n_lat, n_grp)
    everyone = core + x + y + z

    def partner(bit):
        axis, mask = bit
        return {a: (jnp.bitwise_xor(me[a], mask) if a == axis else me[a]) for a in ("grp", "lat")}

    def side(bit):
        axis, mask = bit
        return jnp.bitwise_and(jnp.right_shift(me[axis], mask.bit_length() - 1), 1)

    def send(src, dst, send_sem, recv_sem, bit):
        copy = pltpu.make_async_remote_copy(
            src_ref=src, dst_ref=dst, send_sem=send_sem, recv_sem=recv_sem,
            device_id=partner(bit), device_id_type=MESH)
        copy.start()
        return copy

    barrier = pltpu.get_barrier_semaphore()
    peers = [("lat", m) for m in range(1, n_lat)] + [("grp", m) for m in range(1, n_grp)]
    for bit in peers:
        pl.semaphore_signal(barrier, inc=1, device_id=partner(bit), device_id_type=MESH)
    pl.semaphore_wait(barrier, len(peers))

    half = width // 2
    flows = []
    for p, order in enumerate((x + y + core, y + x + core)):
        flows.append((pl.ds(p * half, half), [mask for _, mask in order]))
    gathers = [{}, {}]

    def forward(p, m, later):
        cols, order = flows[p]
        rank = jnp.bitwise_xor(me["lat"], m)
        src = stream_ref.at[:, cols] if m == 0 else gathered.at[rank, :, cols]
        for mask in later:
            gathers[p][m | mask] = send(
                src, gathered.at[rank, :, cols], gs_sem.at[p, m | mask], gr_sem.at[p, m | mask], ("lat", mask))

    for p in (0, 1):
        forward(p, 0, flows[p][1])

    c = chunk_of(width, 512)
    for at in range(0, width, c):
        weight_t[:, at:at + c] = weight_ref[at:at + c, :].T
    square = (tokens, tokens)
    hits = (lax.broadcasted_iota(jnp.int32, square, 0) == idx_ref[...]).astype(f32)
    count = jnp.sum(hits, axis=1, keepdims=True)
    hits_t[...] = hits.T

    def center(m):
        rank = jnp.bitwise_xor(me["lat"], m)
        for at in range(0, width, c):
            block = stream_ref[:, at:at + c] if m == 0 else gathered[rank, :, at:at + c]
            centered[rank, :, at:at + c] = (block.astype(f32) - dec_ref[:, at:at + c]).astype(bf16)

    def centered_chunk(at, c):
        block = centered[:, :, at:at + c]
        if rows % 16:
            return block.astype(f32).reshape(tokens, c).astype(bf16)
        return block.reshape(tokens, c)

    center(0)
    spans = [[0], [0]]
    for stage in range(len(flows[0][1])):
        fresh = []
        for p in (0, 1):
            for m in spans[p]:
                fresh.append((p, m | flows[p][1][stage]))
        fresh.sort(key=lambda pm: spans[pm[0]].index(pm[1] - flows[pm[0]][1][stage]))
        complete = []
        for p, m in fresh:
            gathers[p][m].wait_recv()
            forward(p, m, flows[p][1][stage + 1:])
            spans[p].append(m)
            if m in spans[1 - p]:
                if stage == len(flows[0][1]) - 1:
                    center(m)
                else:
                    complete.append(m)
        for m in complete:
            center(m)

    preact = jnp.zeros((tokens, weight_ref.shape[1]), f32)
    for at in range(0, width, c):
        preact = preact + jnp.dot(centered_chunk(at, c), weight_ref[at:at + c, :], preferred_element_type=f32)
    preact = preact + enc_ref[...]
    sharp = sharpness * preact
    active32 = (jnp.maximum(sharp, 0.0) + jnp.log1p(jnp.exp(-jnp.abs(sharp)))) / sharpness
    active = active32.astype(bf16)

    parts = split(width // (16 * n), core, x, y, z)
    base, plan = 0, []
    for size, order in parts:
        plan.append((base, size * 16 * n, order))
        base += size * 16 * n
    n_bits = len(everyone)

    def aligned(at):
        return pl.multiple_of(at, 16)

    def term(at, length):
        c = chunk_of(length, 512)
        for k in range(0, length, c):
            here = pl.ds(aligned(at + k), c)
            part[here, :] = lax.dot_general(
                weight_ref[here, :], active, (((1,), (1,)), ((), ())), preferred_element_type=f32).astype(bf16)

    def over(length, most, step):
        c = chunk_of(length, most)
        if length == c:
            step(0, c)
        else:
            @pl.loop(0, length // c)
            def _(k):
                step(aligned(k * c), c)

    where, room = [], 0
    sends = []
    copies = {}
    for p, (start, length, order) in enumerate(plan):
        stay = aligned(start + side(order[0]) * (length // 2))
        go = aligned(start + (1 - side(order[0])) * (length // 2))
        term(go, length // 2)
        spot = room
        room += length // 2
        copies[p] = send(part.at[pl.ds(go, length // 2), :], landed.at[pl.ds(spot, length // 2), :],
                         rs_sem.at[p, 0], rr_sem.at[p, 0], order[0])
        sends.append(copies[p])
        where.append([stay, length // 2, spot])
    for p in range(len(plan)):
        term(where[p][0], where[p][1])

    def turn(stage):
        total = width // c
        for k in range(stage * total // n_bits * c, (stage + 1) * total // n_bits * c, c):
            centered_t[k:k + c, :] = centered_chunk(k, c).T

    turn(0)
    for stage in range(1, n_bits):
        for p, (_, _, order) in enumerate(plan):
            at, length, spot = where[p]
            copies[p].wait_recv()
            now = length // 2
            stay_by = side(order[stage]) * now
            go_by = (1 - side(order[stage])) * now

            def add(by):
                def step(k, c):
                    here = pl.ds(aligned(at + by + k), c)
                    part[here, :] = (part[here, :].astype(f32)
                                     + landed[pl.ds(aligned(spot + by + k), c), :].astype(f32)).astype(bf16)
                over(now, 128, step)

            add(go_by)
            next_spot = room
            room += now
            copies[p] = send(part.at[pl.ds(aligned(at + go_by), now), :], landed.at[pl.ds(next_spot, now), :],
                             rs_sem.at[p, stage], rr_sem.at[p, stage], order[stage])
            sends.append(copies[p])
            add(stay_by)
            where[p] = [aligned(at + stay_by), now, next_spot]
        turn(stage)

    for p, (_, _, order) in enumerate(plan):
        at, length, spot = where[p]
        copies[p].wait_recv()

        def finish(k, c):
            here = pl.ds(aligned(at + k), c)
            total = part[here, :].astype(f32) + landed[pl.ds(aligned(spot + k), c), :].astype(f32)
            grad_t[here, :] = (2.0 * (total - centered_t[here, :].astype(f32))).astype(bf16)
        over(length, 128, finish)

    for stage in reversed(range(n_bits)):
        for p, (_, _, order) in enumerate(plan):
            at, length, _ = where[p]
            if stage < n_bits - 1:
                copies[p].wait_recv()
            region = grad_t.at[pl.ds(at, length), :]
            copies[p] = send(region, region, as_sem.at[p, stage], ar_sem.at[p, stage], order[stage])
            sends.append(copies[p])
            if stage > 0:
                where[p] = [aligned(at - side(order[stage]) * length), 2 * length, 0]

    grad_active_t = jnp.zeros((weight_ref.shape[1], tokens), f32)
    for other in (False, True):
        for p, (start, length, order) in enumerate(plan):
            if other:
                copies[p].wait_recv()
            now = length // 2
            at = start + (1 - side(order[0]) if other else side(order[0])) * now
            c2 = chunk_of(now, 1024)
            for k in range(0, now, c2):
                here = pl.ds(pl.multiple_of(at + k, 128), c2)
                grad_active_t = grad_active_t + jnp.dot(
                    weight_t[:, here], grad_t[here, :], preferred_element_type=f32)
    grad_pre = (grad_active_t.T + penalty) * jax.nn.sigmoid(sharp) * count
    bias_raw = jnp.sum(grad_pre, axis=0, keepdims=True)
    pre16 = grad_pre.astype(bf16)
    drawn = (active32 * count).astype(bf16)
    squares = jnp.zeros((8, weight_ref.shape[1]), f32)
    for k in range(0, width, c):
        block = (jnp.dot(centered_t[k:k + c, :], pre16, preferred_element_type=f32)
                 + jnp.dot(grad_t[k:k + c, :], drawn, preferred_element_type=f32))
        raw[k:k + c, :] = block.astype(bf16)
        squares = squares + jnp.sum((block * block).reshape(c // 8, 8, block.shape[1]), axis=0)
    first = lax.broadcasted_iota(jnp.int32, squares.shape, 0) == 0
    squares = squares + jnp.where(first, bias_raw * bias_raw, 0.0)

    lat_tiles[me["lat"]] = squares
    arrivals = []
    for m in range(1, n_lat):
        slot = lat_tiles.at[me["lat"]]
        arrivals.append(send(slot, slot, ls_sem.at[m], lr_sem.at[m], ("lat", m)))
    out_copy = pltpu.make_async_copy(raw, raw_ref, out_sem)
    out_copy.start()

    pick = hits_t[pl.ds(pl.multiple_of(me["lat"] * rows, 8), rows), :].astype(bf16)

    def recon(ks):
        for k in ks:
            rows_of = lax.dot_general(pick, grad_t[k:k + c, :], (((1,), (1,)), ((), ())), preferred_element_type=f32)
            err_ref[:, k:k + c] = (0.5 * rows_of).astype(bf16)

    recon(range(0, half, c))
    for copy in arrivals:
        copy.wait_recv()
    sends += arrivals
    grp_tiles[me["grp"]] = jnp.sum(lat_tiles[...], axis=0)
    arrivals = []
    for m in range(1, n_grp):
        slot = grp_tiles.at[me["grp"]]
        arrivals.append(send(slot, slot, zs_sem.at[m], zr_sem.at[m], ("grp", m)))
    recon(range(half, width, c))
    for copy in arrivals:
        copy.wait_recv()
    sends += arrivals
    total = jnp.sum(grp_tiles[...])
    entries = (width + 1) * weight_ref.shape[1] * n
    mean = jnp.full((1, weight_ref.shape[1]), total / entries + epsilon, f32)
    factor_ref[...] = jnp.minimum(1.0, 1.0 / jnp.sqrt(mean))
    bias_ref[...] = bias_raw

    out_copy.wait()
    for copy in sends:
        copy.wait_send()
    for p in (0, 1):
        for m in sorted(gathers[p]):
            gathers[p][m].wait_send()


def body(n_lat, n_grp, stream, batch_index, weight, enc_bias, dec_bias):
    rows, width = stream.shape
    tokens = batch_index.shape[0]
    latents = weight.shape[1]
    n_bits = (n_lat * n_grp).bit_length() - 1
    n_parts = len(split(width // (16 * n_lat * n_grp), *bit_orders(n_lat, n_grp)))
    vmem = pl.BlockSpec(memory_space=pltpu.VMEM)
    dma = pltpu.SemaphoreType.DMA
    raw, bias_raw, factor, error = pl.pallas_call(
        functools.partial(kernel, n_lat, n_grp, n_parts),
        out_shape=(
            jax.ShapeDtypeStruct(weight.shape, bf16),
            jax.ShapeDtypeStruct((1, latents), f32),
            jax.ShapeDtypeStruct((1, latents), f32),
            jax.ShapeDtypeStruct((rows, width), bf16),
        ),
        in_specs=[vmem] * 5,
        out_specs=(pl.BlockSpec(memory_space=pl.ANY), vmem, vmem, vmem),
        scratch_shapes=[
            pltpu.VMEM((n_lat, rows, width), bf16),
            pltpu.VMEM((n_lat, rows, width), bf16),
            pltpu.VMEM((width, tokens), bf16),
            pltpu.VMEM((latents, width), bf16),
            pltpu.VMEM((width, tokens), bf16),
            pltpu.VMEM((width, tokens), bf16),
            pltpu.VMEM((width, tokens), bf16),
            pltpu.VMEM((width, latents), bf16),
            pltpu.VMEM((tokens, tokens), f32),
            pltpu.VMEM((n_lat, 8, latents), f32),
            pltpu.VMEM((n_grp, 8, latents), f32),
            dma((2, n_lat)),
            dma((2, n_lat)),
            dma((n_parts, n_bits)),
            dma((n_parts, n_bits)),
            dma((n_parts, n_bits)),
            dma((n_parts, n_bits)),
            dma((n_lat,)),
            dma((n_lat,)),
            dma((n_grp,)),
            dma((n_grp,)),
            dma,
        ],
        compiler_params=pltpu.CompilerParams(
            collective_id=0, has_side_effects=True, vmem_limit_bytes=56 * 1024 * 1024),
        cost_estimate=pl.CostEstimate(
            flops=2 * tokens * width * latents * 5, bytes_accessed=8 * width * latents, transcendentals=0),
    )(
        stream,
        batch_index.reshape(1, tokens),
        weight,
        enc_bias.reshape(1, latents),
        dec_bias.reshape(1, width),
    )
    weight_grad = (raw.astype(f32) * factor).astype(bf16)
    return weight_grad, (bias_raw * factor).reshape(latents), error


def solution(mesh):
    return jax.shard_map(
        functools.partial(body, mesh.shape["lat"], mesh.shape["grp"]),
        mesh=mesh,
        in_specs=(P("lat", None), P(), P(None, ("grp", "lat")), P(("grp", "lat")), P()),
        out_specs=(P(None, ("grp", "lat")), P(("grp", "lat")), P("lat", None)),
        check_vma=False,
    )
```
